32 devices in a mesh: pipe: 4 (over y, core), expert: 8 (over z, x).
Axes of the slice: x: 2, y: 2, z: 4, core: 2. Of those that a mesh axis runs over, the one named last changes fastest.
Arguments:
- acts_first: bfloat16 [4, 1024, 3584], P('pipe', 'expert'), may hold values from -6 to 6
- route_first: int32 [4, 1024, 1], P('pipe', 'expert'), may hold values from 0 to 1; in each aligned block of 128 rows (0 to 127, 128 to 255, ..., all dimensions but the last counted through in order) at most 96 rows name the same one
- weight_first: float32 [4, 1024, 1], P('pipe', 'expert'), may hold values from 0.3 to 1.5
- acts_second: bfloat16 [4, 1024, 3584], P('pipe', 'expert'), may hold values from -6 to 6
- grad_second: bfloat16 [4, 1024, 3584], P('pipe', 'expert'), may hold values from -6 to 6
- route_second: int32 [4, 1024, 1], P('pipe', 'expert'), may hold values from 0 to 1; in each aligned block of 128 rows (0 to 127, 128 to 255, ..., all dimensions but the last counted through in order) at most 96 rows name the same one
- weight_second: float32 [4, 1024, 1], P('pipe', 'expert'), may hold values from 0.3 to 1.5
- gain_first: float32 [4, 3584], P('pipe'), may hold values from 0.5 to 1.5
- up_first: bfloat16 [4, 3584, 2048], P('pipe', None, 'expert'), may hold values from -0.09375 to 0.09375
- down_first: bfloat16 [4, 2048, 3584], P('pipe', 'expert'), may hold values from -0.1875 to 0.1875
- gain_second: float32 [4, 3584], P('pipe'), may hold values from 0.5 to 1.5
- up_second: bfloat16 [4, 3584, 2048], P('pipe', None, 'expert'), may hold values from -0.09375 to 0.09375
- down_second: bfloat16 [4, 2048, 3584], P('pipe', 'expert'), may hold values from -0.1875 to 0.1875
Outputs:
- next_first: bfloat16 [4, 1024, 3584], P('pipe', 'expert')
- next_grad: bfloat16 [4, 1024, 3584], P('pipe', 'expert')
The draws below stay inside these ranges and needn't reach their ends.
Inputs may be any that keep to these rules, and one draw needn't show every extreme that they name: `route_first`: among the 128 tokens of one device (an aligned block of 128 tokens at one pipe index), at most 96 choose the same expert, and some device has exactly 96 on one expert. `route_second`: among the 128 tokens of one device (an aligned block of 128 tokens at one pipe index), at most 96 choose the same expert, and some device has exactly 96 on one expert.
All inputs are finite; a program needn't handle non-finite values.
Results may differ from the reference program's by a relative error of at most 0.0054.
Values may be sent and summed in bfloat16 or wider, within the bound.
No kernel may reach another device: no remote copies, remote signals or barrier semaphores. Data moves between devices by JAX's collectives and lax.ppermute only.
A program may use at most 128 MiB of HBM per device.

```python
import math
import jax
import jax.numpy as jnp
import numpy as np
from jax import lax

D = 3584
FFE = 1024
SPLIT = 4
TOPK = 1
TOK_DEV = 128
EXPERTS = 2
HID_DEV = 256
CAP = 96
TOKENS = 1024
N_PIPE = 4
N_EXPERT = 8


def shard_levels(key, extent, shards, low, largest):
    level, own = 1.0, jax.random.fold_in(key, 6)
    for dim, blocks in shards:
        steps = jnp.exp(jax.random.uniform(jax.random.fold_in(own, dim), (blocks,), jnp.float32, low / len(shards), largest / len(shards)))
        level = level * jnp.repeat(steps, extent[dim] // blocks).reshape([-1 if axis == dim else 1 for axis in range(len(extent))])
    return level


def assign_block(key, own, number, rows, count, top, reach, lean):
    ranking = jax.random.permutation(key, count)
    heavy_load, ordinary = portions_of(count, rows * top, reach, lean, True), portions_of(count, rows * top, reach, lean, False)
    places = jnp.arange(count)

    def named(lengths, offset_by):
        used = int((lengths > 0).sum())
        fixed = max(1, used // 4)
        moved = fixed + (places - fixed + offset_by * (used - fixed)) % max(1, count - fixed)
        return jnp.zeros((count,), jnp.int32).at[ranking[jnp.where(places < fixed, places, moved)]].set(jnp.asarray(lengths, jnp.int32))

    lengths = jnp.where(number % 4 == 0, named(heavy_load, number // 4), named(ordinary, number - number // 4 - 1))
    mixed = jax.random.permutation(jax.random.fold_in(own, 3), count)
    source_of, sink = mixed[0:count // 2 * 2:2], mixed[1:count // 2 * 2:2]
    margin = jnp.minimum(lengths[source_of] - 1, reach - lengths[sink]) // 2
    margin = jnp.where((source_of == ranking[0]) | (sink == ranking[0]) | (lengths[sink] == 0), 0, jnp.maximum(margin, 0))
    moved = jax.random.randint(jax.random.fold_in(own, 4), (count // 2,), 0, 1 << 20) % (margin + 1)
    lengths = lengths.at[source_of].add(-moved).at[sink].add(moved)
    members = jnp.searchsorted(jnp.cumsum(lengths), jnp.arange(rows * top), side="right").astype(jnp.int32)
    listing = members.reshape(top, rows).T
    listing = listing[jax.random.permutation(jax.random.fold_in(own, 1), rows)]
    offset_by = jax.random.randint(jax.random.fold_in(own, 2), (rows, 1), 0, top)
    return jnp.take_along_axis(listing, (jnp.arange(top)[None, :] + offset_by) % top, axis=1)


def portions_of(count, total, most, skew, full):
    portions = [(1 << 20) // math.isqrt(rank ** skew) + 1 for rank in range(1, count + 1)]
    largest = most if full else min(most, max(-(-total // count), total * portions[0] // sum(portions)))
    least = 1 if total - largest >= count - 1 else 0
    holding, spare = [largest] + [least] * (count - 1), total - largest - least * (count - 1)
    while spare > 0:
        candidates = [i for i in range(1, count) if holding[i] < largest] or [i for i in range(1, count) if holding[i] < most]
        pool, budget = sum([portions[i] for i in candidates]), spare
        for i in candidates:
            extra = min(most - holding[i], max(1, budget * portions[i] // pool), spare)
            holding[i] = holding[i] + extra
            spare = spare - extra
    return np.array(holding)


def scatter_about(stream_key, extent, spread, bound, shards=(), held_as=jnp.bfloat16):
    drawn = spread * jax.random.normal(stream_key, extent, jnp.float32)
    if shards:
        drawn = drawn * shard_levels(stream_key, extent, shards, -0.22, 0.18)
    return jnp.clip(drawn, -bound, bound).astype(held_as)


def setup_inputs(seed: int = 0) -> dict:
    arg_keys = jax.random.split(jax.random.key(seed), 14)
    acts_first = scatter_about(arg_keys[0], (N_PIPE, TOKENS, D), 1.0, 6.0, ((0, 4), (1, 8)))
    route_first_keys = jax.random.split(jax.random.fold_in(arg_keys[1], 1), N_PIPE * TOKENS // TOK_DEV)
    route_first_turns = jax.random.permutation(jax.random.fold_in(arg_keys[1], 3), N_PIPE * TOKENS // TOK_DEV)
    route_first = jax.vmap(lambda own, number: assign_block(jax.random.fold_in(arg_keys[1], 2), own, number, TOK_DEV, EXPERTS, TOPK, CAP, 2))(route_first_keys, route_first_turns).reshape((N_PIPE, TOKENS, TOPK))
    weight_first = jnp.clip(jnp.exp(math.log(1.5) - 1.60943787 * jax.random.uniform(arg_keys[2], (N_PIPE, TOKENS, TOPK), jnp.float32) ** shard_levels(arg_keys[2], (N_PIPE, TOKENS, TOPK), ((0, 4), (1, 8)), -0.2, 0.2)), 0.3, 1.5)
    acts_second = scatter_about(arg_keys[3], (N_PIPE, TOKENS, D), 1.0, 6.0, ((0, 4), (1, 8)))
    grad_second = scatter_about(arg_keys[4], (N_PIPE, TOKENS, D), 1.0, 6.0, ((0, 4), (1, 8)))
    route_second_keys = jax.random.split(jax.random.fold_in(arg_keys[5], 1), N_PIPE * TOKENS // TOK_DEV)
    route_second_turns = jax.random.permutation(jax.random.fold_in(arg_keys[5], 3), N_PIPE * TOKENS // TOK_DEV)
    route_second = jax.vmap(lambda own, number: assign_block(jax.random.fold_in(arg_keys[5], 2), own, number, TOK_DEV, EXPERTS, TOPK, CAP, 2))(route_second_keys, route_second_turns).reshape((N_PIPE, TOKENS, TOPK))
    weight_second = jnp.clip(jnp.exp(math.log(1.5) - 1.60943787 * jax.random.uniform(arg_keys[6], (N_PIPE, TOKENS, TOPK), jnp.float32) ** shard_levels(arg_keys[6], (N_PIPE, TOKENS, TOPK), ((0, 4), (1, 8)), -0.2, 0.2)), 0.3, 1.5)
    gain_first = jnp.clip(1.0 + 0.1 * jax.random.normal(arg_keys[7], (N_PIPE, D), jnp.float32), 0.5, 1.5)
    up_first = scatter_about(arg_keys[8], (N_PIPE, D, EXPERTS * FFE), D ** -0.5, 0.09375, ((0, 4), (2, 8)))
    down_first = scatter_about(arg_keys[9], (N_PIPE, EXPERTS * FFE, D), FFE ** -0.5, 0.1875, ((0, 4), (1, 8)))
    gain_second = jnp.clip(1.0 + 0.1 * jax.random.normal(arg_keys[10], (N_PIPE, D), jnp.float32), 0.5, 1.5)
    up_second = scatter_about(arg_keys[11], (N_PIPE, D, EXPERTS * FFE), D ** -0.5, 0.09375, ((0, 4), (2, 8)))
    down_second = scatter_about(arg_keys[12], (N_PIPE, EXPERTS * FFE, D), FFE ** -0.5, 0.1875, ((0, 4), (1, 8)))
    return dict(acts_first=acts_first, route_first=route_first, weight_first=weight_first, acts_second=acts_second, grad_second=grad_second, route_second=route_second, weight_second=weight_second, gain_first=gain_first, up_first=up_first, down_first=down_first, gain_second=gain_second, up_second=up_second, down_second=down_second)


def normalize(acts, gain_row):
    values = acts.astype(jnp.float32)
    inverse_rms = lax.rsqrt(lax.optimization_barrier(jnp.mean(values * values, axis=-1, keepdims=True)) + 1e-06)
    return (values, inverse_rms, (values * inverse_rms * gain_row).astype(jnp.bfloat16))

def positions(route_ids):
    local_ids = route_ids.reshape(N_EXPERT, TOK_DEV).astype(jnp.int32)
    onehot = (local_ids[:, :, None] == jnp.arange(EXPERTS, dtype=jnp.int32)[None, None, :]).astype(jnp.int32)
    before = jnp.cumsum(onehot, axis=1, dtype=jnp.int32) - onehot
    slot_index = lax.optimization_barrier(jnp.sum(before * onehot, axis=2, dtype=jnp.int32))
    return (local_ids * CAP + slot_index).astype(jnp.int32)

def scatter_rows(source_rows, where_rows):

    def place_rows(rows_one, where_one):
        return jnp.zeros((EXPERTS * CAP, D), rows_one.dtype).at[where_one].set(rows_one)
    placed = jax.vmap(place_rows)(source_rows.reshape(N_EXPERT, TOK_DEV, D), where_rows)
    return placed.reshape(N_EXPERT, EXPERTS, CAP, D).transpose(1, 0, 2, 3).reshape(EXPERTS, N_EXPERT * CAP, D)

def collect_rows(results, where_rows):
    placed = results.reshape(EXPERTS, N_EXPERT, CAP, D).transpose(1, 0, 2, 3).reshape(N_EXPERT, EXPERTS * CAP, D)
    picked = jax.vmap(lambda table, where_one: table[where_one])(placed, where_rows)
    return picked.reshape(N_EXPERT * TOK_DEV, D)

def round_sum(partials):
    rounded = lax.optimization_barrier(partials.astype(jnp.bfloat16))
    return lax.optimization_barrier(jnp.sum(rounded.astype(jnp.float32), axis=0))

def expert_forward(section_items):
    packed_rows, up_block, down_block = section_items
    row_total = packed_rows.shape[0]
    upper_in = jnp.dot(packed_rows, up_block, preferred_element_type=jnp.float32)
    hidden = jax.nn.silu(upper_in).astype(jnp.bfloat16)
    partials = jnp.einsum('rqh,qhd->qrd', hidden.reshape(row_total, SPLIT, HID_DEV).astype(jnp.float32), down_block.reshape(SPLIT, HID_DEV, D).astype(jnp.float32))
    return round_sum(partials)

def expert_backward(section_items):
    packed_rows, grad_rows, up_block, down_block = section_items
    row_total = packed_rows.shape[0]
    upper_in = jnp.dot(packed_rows, up_block, preferred_element_type=jnp.float32)
    sigmoid_up = jax.nn.sigmoid(upper_in)
    back_hidden = jnp.dot(grad_rows, down_block.T, preferred_element_type=jnp.float32)
    back_upper = (back_hidden * sigmoid_up * (1.0 + upper_in * (1.0 - sigmoid_up))).astype(jnp.bfloat16)
    partials = jnp.einsum('rqh,dqh->qrd', back_upper.reshape(row_total, SPLIT, HID_DEV).astype(jnp.float32), up_block.reshape(D, SPLIT, HID_DEV).astype(jnp.float32))
    return round_sum(partials)

def one_section(section_items):
    acts_a, route_a, weight_a, acts_b, grad_b, route_b, weight_b, gain_a, up_a, down_a, gain_b, up_b, down_b = section_items
    values_a, inverse_a, normed_a = normalize(acts_a, gain_a)
    values_b, inverse_b, normed_b = normalize(acts_b, gain_b)
    scaled_grad = (weight_b * grad_b.astype(jnp.float32)).astype(jnp.bfloat16)
    where_a = positions(route_a[:, 0])
    where_b = positions(route_b[:, 0])
    rows_a = scatter_rows(normed_a, where_a)
    rows_b = scatter_rows(normed_b, where_b)
    grads_b = scatter_rows(scaled_grad, where_b)
    up_blocks_a = up_a.reshape(D, EXPERTS, FFE).transpose(1, 0, 2)
    down_blocks_a = down_a.reshape(EXPERTS, FFE, D)
    up_blocks_b = up_b.reshape(D, EXPERTS, FFE).transpose(1, 0, 2)
    down_blocks_b = down_b.reshape(EXPERTS, FFE, D)
    out_a = lax.map(expert_forward, (rows_a, up_blocks_a, down_blocks_a))
    back_b = lax.map(expert_backward, (rows_b, grads_b, up_blocks_b, down_blocks_b))
    expert_a = collect_rows(out_a, where_a)
    mixed_first = (values_a + weight_a * expert_a).astype(jnp.bfloat16)
    back_normed = collect_rows(back_b, where_b)
    gained_back = gain_b * back_normed
    scale_cubed = inverse_b * inverse_b * inverse_b
    grad_acts = grad_b.astype(jnp.float32) + inverse_b * gained_back - values_b * scale_cubed * lax.optimization_barrier(jnp.mean(values_b * gained_back, axis=-1, keepdims=True))
    return (mixed_first, grad_acts.astype(jnp.bfloat16))

def reference(acts_first, route_first, weight_first, acts_second, grad_second, route_second, weight_second, gain_first, up_first, down_first, gain_second, up_second, down_second):
    mixed_all, grad_all = lax.map(one_section, (acts_first, route_first, weight_first, acts_second, grad_second, route_second, weight_second, gain_first, up_first, down_first, gain_second, up_second, down_second))
    return (jnp.roll(mixed_all, 1, axis=0), jnp.roll(grad_all, 1, axis=0))
```

```python
import functools

import jax
import jax.numpy as jnp
from jax import lax
from jax.experimental import pallas as pl
from jax.experimental.pallas import tpu as pltpu
from jax.sharding import PartitionSpec as P

SPLIT = 4
VMEM_LIMIT = 40 * 1024 * 1024
PARAMS = pltpu.CompilerParams(vmem_limit_bytes=VMEM_LIMIT)
WHOLE = pl.BlockSpec(memory_space=pltpu.VMEM)


def shifted(block, axis, distance):
    devices = range(lax.axis_size(axis))
    route = [((i - distance) % len(devices), i) for i in devices]
    return lax.ppermute(block, axis, route)


def swapped(block, bit):
    return lax.ppermute(block, "expert", [(i, i ^ bit) for i in range(lax.axis_size("expert"))])


def to_group(block, distance):
    owners = lax.axis_size("expert")
    return lax.ppermute(
        block, "expert", [(i, (i + distance * SPLIT) % owners) for i in range(owners)]
    )


def width_step(width):
    lanes = width // 128
    return 128 * max(n for n in range(1, 9) if lanes % n == 0)


def dot(left, right, left_dim, right_dim):
    return lax.dot_general(
        left, right, (((left_dim,), (right_dim,)), ((), ())), preferred_element_type=jnp.float32
    )


def slot_numbers(relative):
    tokens = relative.shape[0]
    chosen = relative == lax.broadcasted_iota(jnp.int32, (tokens, 128), 1)
    onehot = jnp.where(chosen, 1.0, 0.0)
    earlier = lax.broadcasted_iota(jnp.int32, (tokens, tokens), 1) < lax.broadcasted_iota(
        jnp.int32, (tokens, tokens), 0
    )
    before = dot(
        jnp.where(earlier, 1.0, 0.0).astype(jnp.bfloat16), onehot.astype(jnp.bfloat16), 1, 0
    )
    return jnp.sum(before * onehot, axis=1, keepdims=True).astype(jnp.int32)


def placement(relative, slots, group, capacity):
    tokens = relative.shape[0]
    columns = lax.broadcasted_iota(jnp.int32, (tokens, capacity), 1)
    inside = jnp.where(relative == group, slots, -1)
    return jnp.where(inside == columns, 1.0, 0.0).astype(jnp.bfloat16)


def inverse_rms_of(acts_ref, step):
    width = acts_ref.shape[1]
    squares = 0.0
    for start in range(0, width, step):
        values = acts_ref[:, start : start + step].astype(jnp.float32)
        squares = squares + jnp.sum(values * values, axis=1, keepdims=True)
    return lax.rsqrt(squares / width + 1e-06)


def prepare_first_body(groups, capacity, step, relative_ref, acts_ref, gain_ref, stay_ref, cross_ref):
    relative = relative_ref[...]
    slots = slot_numbers(relative)
    places = [placement(relative, slots, k, capacity) for k in range(groups)]
    inverse_rms = inverse_rms_of(acts_ref, step)
    for start in range(0, acts_ref.shape[1], step):
        part = slice(start, start + step)
        normed = acts_ref[:, part].astype(jnp.float32) * inverse_rms * gain_ref[:, part]
        normed = normed.astype(jnp.bfloat16)
        stay_ref[:, part] = dot(places[0], normed, 0, 0).astype(jnp.bfloat16)
        for k in range(1, groups):
            cross_ref[k - 1, :, part] = dot(places[k], normed, 0, 0).astype(jnp.bfloat16)


def prepare_second_body(
    groups,
    capacity,
    step,
    relative_ref,
    weight_ref,
    acts_ref,
    grad_ref,
    gain_ref,
    stay_ref,
    cross_ref,
):
    relative = relative_ref[...]
    slots = slot_numbers(relative)
    places = [placement(relative, slots, k, capacity) for k in range(groups)]
    inverse_rms = inverse_rms_of(acts_ref, step)
    for start in range(0, acts_ref.shape[1], step):
        part = slice(start, start + step)
        normed = acts_ref[:, part].astype(jnp.float32) * inverse_rms * gain_ref[:, part]
        scaled = weight_ref[...] * grad_ref[:, part].astype(jnp.float32)
        for row, values in enumerate((normed.astype(jnp.bfloat16), scaled.astype(jnp.bfloat16))):
            stay_ref[row, :, part] = dot(places[0], values, 0, 0).astype(jnp.bfloat16)
            for k in range(1, groups):
                cross_ref[k - 1, row, :, part] = dot(places[k], values, 0, 0).astype(jnp.bfloat16)


def backward_hidden_body(pieces, *refs):
    rows_refs = refs[:pieces]
    up_refs, down_refs = refs[pieces : pieces + 2], refs[pieces + 2 : pieces + 4]
    back_ref, upper_total, hidden_total = refs[pieces + 4 :]
    step, steps = pl.program_id(0), pl.num_programs(0)
    normed = jnp.concatenate([ref[0] for ref in rows_refs], axis=0)
    scaled = jnp.concatenate([ref[1] for ref in rows_refs], axis=0)
    hidden = up_refs[0].shape[1]

    @pl.when(step == 0)
    def _():
        upper_total[...] = jnp.zeros_like(upper_total)
        hidden_total[...] = jnp.zeros_like(hidden_total)

    for lane in range(2):
        part = slice(lane * hidden, (lane + 1) * hidden)
        upper_total[:, part] += dot(normed, up_refs[lane][...], 1, 0)
        hidden_total[:, part] += dot(scaled, down_refs[lane][...], 1, 1)

    @pl.when(step == steps - 1)
    def _():
        upper = upper_total[...]
        sigmoid = jax.nn.sigmoid(upper)
        back = hidden_total[...] * sigmoid * (1.0 + upper * (1.0 - sigmoid))
        back_ref[...] = back.astype(jnp.bfloat16)


def forward_hidden_body(pieces, *refs):
    rows_refs = refs[:pieces]
    up_refs = refs[pieces : pieces + 2]
    hidden_ref, upper_total = refs[pieces + 2 :]
    step, steps = pl.program_id(0), pl.num_programs(0)
    normed = jnp.concatenate([ref[...] for ref in rows_refs], axis=0)
    hidden = up_refs[0].shape[1]

    @pl.when(step == 0)
    def _():
        upper_total[...] = jnp.zeros_like(upper_total)

    for lane in range(2):
        part = slice(lane * hidden, (lane + 1) * hidden)
        upper_total[:, part] += dot(normed, up_refs[lane][...], 1, 0)

    @pl.when(step == steps - 1)
    def _():
        upper = upper_total[...]
        hidden_ref[...] = (upper * jax.nn.sigmoid(upper)).astype(jnp.bfloat16)


def spread_body(weights_dim, own_rows, hidden_ref, one_ref, other_ref, own_ref, away_ref):
    hidden = one_ref.shape[1 - weights_dim] if weights_dim == 0 else one_ref.shape[0]
    hidden = hidden_ref.shape[1] // 2
    contract = 1 if weights_dim == 0 else 0
    total = dot(hidden_ref[:, :hidden], one_ref[...], 1, contract)
    total = total + dot(hidden_ref[:, hidden:], other_ref[...], 1, contract)
    own_ref[...] = total[:own_rows]
    away_ref[...] = total[own_rows:].astype(jnp.bfloat16)


def spread(hidden_rows, one, other, weights_dim, first, length, step):
    own_rows = hidden_rows.shape[0] // 2
    offset = first // step
    if weights_dim == 0:
        block, index = (step, one.shape[1]), lambda j: (j + offset, 0)
    else:
        block, index = (one.shape[0], step), lambda j: (0, j + offset)
    return pl.pallas_call(
        functools.partial(spread_body, weights_dim, own_rows),
        grid=(length // step,),
        in_specs=[
            pl.BlockSpec(hidden_rows.shape, lambda j: (0, 0)),
            pl.BlockSpec(block, index),
            pl.BlockSpec(block, index),
        ],
        out_specs=[pl.BlockSpec((own_rows, step), lambda j: (0, j))] * 2,
        out_shape=[
            jax.ShapeDtypeStruct((own_rows, length), jnp.float32),
            jax.ShapeDtypeStruct((own_rows, length), jnp.bfloat16),
        ],
        compiler_params=PARAMS,
    )(hidden_rows, one, other)


def collected(relative, groups, capacity, own, partner, returned):
    slots = slot_numbers(relative)
    stay = own + partner.astype(jnp.float32)
    high = stay.astype(jnp.bfloat16)
    low = (stay - high.astype(jnp.float32)).astype(jnp.bfloat16)
    here = placement(relative, slots, 0, capacity)
    total = dot(here, high, 1, 0) + dot(here, low, 1, 0)
    away = (groups - 1) * capacity
    columns = lax.broadcasted_iota(jnp.int32, (relative.shape[0], away), 1)
    inside = jnp.where(relative > 0, (relative - 1) * capacity + slots, -1)
    there = jnp.where(inside == columns, 1.0, 0.0).astype(jnp.bfloat16)
    return total + dot(there, returned, 1, 0)


def finish_first_body(
    groups, capacity, relative_ref, weight_ref, acts_ref, own_ref, partner_ref, returned_ref, out_ref
):
    total = collected(
        relative_ref[...], groups, capacity, own_ref[...], partner_ref[...], returned_ref[...]
    )
    out_ref[...] = (acts_ref[...].astype(jnp.float32) + weight_ref[...] * total).astype(
        jnp.bfloat16
    )


def finish_second_body(
    groups,
    capacity,
    step,
    relative_ref,
    acts_ref,
    grad_ref,
    gain_ref,
    own_ref,
    partner_ref,
    returned_ref,
    out_ref,
    gained,
):
    width = acts_ref.shape[1]
    relative = relative_ref[...]
    inverse_rms = inverse_rms_of(acts_ref, step)
    along = 0.0
    for start in range(0, width, step):
        part = slice(start, start + step)
        total = collected(
            relative, groups, capacity, own_ref[:, part], partner_ref[:, part], returned_ref[:, part]
        )
        total = gain_ref[:, part] * total
        gained[:, part] = total
        along = along + jnp.sum(
            acts_ref[:, part].astype(jnp.float32) * total, axis=1, keepdims=True
        )
    scale = inverse_rms * inverse_rms * inverse_rms * (along / width)
    for start in range(0, width, step):
        part = slice(start, start + step)
        values = acts_ref[:, part].astype(jnp.float32)
        out = grad_ref[:, part].astype(jnp.float32) + inverse_rms * gained[:, part] - values * scale
        out_ref[:, part] = out.astype(jnp.bfloat16)


def rows_blocks(arrays, step):
    specs = []
    for array in arrays:
        lead = array.shape[:-1]
        specs.append(pl.BlockSpec((*lead, step), lambda j, zeros=(0,) * len(lead): (*zeros, j)))
    return specs


def per_device(
    acts_first,
    route_first,
    weight_first,
    acts_second,
    grad_second,
    route_second,
    weight_second,
    gain_first,
    up_first,
    down_first,
    gain_second,
    up_second,
    down_second,
):
    owners = lax.axis_size("expert")
    groups = owners // SPLIT
    tokens, width = acts_first.shape[1:]
    capacity = 3 * tokens * SPLIT // (2 * owners)
    away = (groups - 1) * capacity
    step = width_step(width)
    hidden = up_first.shape[2]
    bf16 = jnp.bfloat16
    group = lax.axis_index("expert") // SPLIT
    relative_first = (route_first[0] - group + groups) % groups
    relative_second = (route_second[0] - group + groups) % groups

    down_second_other = swapped(down_second[0], 2)

    stay_second, cross_second = pl.pallas_call(
        functools.partial(prepare_second_body, groups, capacity, step),
        in_specs=[WHOLE] * 5,
        out_specs=[WHOLE] * 2,
        out_shape=[
            jax.ShapeDtypeStruct((2, capacity, width), bf16),
            jax.ShapeDtypeStruct((groups - 1, 2, capacity, width), bf16),
        ],
        compiler_params=PARAMS,
    )(relative_second, weight_second[0], acts_second[0], grad_second[0], gain_second)
    came_second = [to_group(cross_second[k - 1], k) for k in range(1, groups)]
    came_second = came_second[0] if groups == 2 else jnp.concatenate(came_second, axis=1)
    stay_second_other = swapped(stay_second, 1)
    up_second_other = swapped(up_second[0], 2)
    up_first_other = swapped(up_first[0], 1)

    stay_first, cross_first = pl.pallas_call(
        functools.partial(prepare_first_body, groups, capacity, step),
        in_specs=[WHOLE] * 3,
        out_specs=[WHOLE] * 2,
        out_shape=[
            jax.ShapeDtypeStruct((capacity, width), bf16),
            jax.ShapeDtypeStruct((groups - 1, capacity, width), bf16),
        ],
        compiler_params=PARAMS,
    )(relative_first, acts_first[0], gain_first)
    came_first = [to_group(cross_first[k - 1], k) for k in range(1, groups)]
    came_first = came_first[0] if groups == 2 else jnp.concatenate(came_first, axis=0)
    came_second_other = swapped(came_second, 1)
    stay_first_other = swapped(stay_first, 2)
    came_first_other = swapped(came_first, 2)
    down_first_other = swapped(down_first[0], 1)

    rows = [stay_second, came_second, stay_second_other, came_second_other]
    if capacity % 16:
        rows = [jnp.concatenate(rows, axis=1)]
    both = 2 * (capacity + away)
    back_upper = pl.pallas_call(
        functools.partial(backward_hidden_body, len(rows)),
        grid=(width // step,),
        in_specs=rows_blocks(rows, step)
        + [pl.BlockSpec((step, hidden), lambda j: (j, 0))] * 2
        + [pl.BlockSpec((hidden, step), lambda j: (0, j))] * 2,
        out_specs=pl.BlockSpec((both, 2 * hidden), lambda j: (0, 0)),
        out_shape=jax.ShapeDtypeStruct((both, 2 * hidden), bf16),
        scratch_shapes=[pltpu.VMEM((both, 2 * hidden), jnp.float32)] * 2,
        compiler_params=PARAMS,
    )(*rows, up_second[0], up_second_other, down_second[0], down_second_other)
    own_second, send_second = spread(
        back_upper, up_second[0], up_second_other, 0, 0, width, step
    )
    came_part = swapped(send_second[capacity:], 1)
    stay_part = swapped(send_second[:capacity], 1)
    back = (own_second[capacity:] + came_part.astype(jnp.float32)).astype(bf16)
    returned = [
        to_group(back[(k - 1) * capacity : k * capacity], groups - k) for k in range(1, groups)
    ]
    returned = returned[0] if groups == 2 else jnp.concatenate(returned, axis=0)
    grad_acts = pl.pallas_call(
        functools.partial(finish_second_body, groups, capacity, step),
        in_specs=[WHOLE] * 7,
        out_specs=WHOLE,
        out_shape=jax.ShapeDtypeStruct((tokens, width), bf16),
        scratch_shapes=[pltpu.VMEM((tokens, width), jnp.float32)],
        compiler_params=PARAMS,
    )(
        relative_second,
        acts_second[0],
        grad_second[0],
        gain_second,
        own_second[:capacity],
        stay_part,
        returned,
    )
    next_grad = shifted(grad_acts, "pipe", 1)

    rows = [stay_first, came_first, stay_first_other, came_first_other]
    if capacity % 16:
        rows = [jnp.concatenate(rows, axis=0)]
    hidden_first = pl.pallas_call(
        functools.partial(forward_hidden_body, len(rows)),
        grid=(width // step,),
        in_specs=rows_blocks(rows, step) + [pl.BlockSpec((step, hidden), lambda j: (j, 0))] * 2,
        out_specs=pl.BlockSpec((both, 2 * hidden), lambda j: (0, 0)),
        out_shape=jax.ShapeDtypeStruct((both, 2 * hidden), bf16),
        scratch_shapes=[pltpu.VMEM((both, 2 * hidden), jnp.float32)],
        compiler_params=PARAMS,
    )(*rows, up_first[0], up_first_other)
    next_parts = []
    parts = 2 if (width // step) % 2 == 0 else 1
    length = width // parts
    for first in range(0, width, length):
        own_first, send_first = spread(
            hidden_first, down_first[0], down_first_other, 1, first, length, step
        )
        came_part = swapped(send_first[capacity:], 2)
        stay_part = swapped(send_first[:capacity], 2)
        back = (own_first[capacity:] + came_part.astype(jnp.float32)).astype(bf16)
        returned = [
            to_group(back[(k - 1) * capacity : k * capacity], groups - k)
            for k in range(1, groups)
        ]
        returned = returned[0] if groups == 2 else jnp.concatenate(returned, axis=0)
        mixed = pl.pallas_call(
            functools.partial(finish_first_body, groups, capacity),
            in_specs=[WHOLE] * 6,
            out_specs=WHOLE,
            out_shape=jax.ShapeDtypeStruct((tokens, length), bf16),
            compiler_params=PARAMS,
        )(
            relative_first,
            weight_first[0],
            acts_first[0][:, first : first + length],
            own_first[:capacity],
            stay_part,
            returned,
        )
        next_parts.append(shifted(mixed, "pipe", 1))
    next_first = next_parts[0] if parts == 1 else jnp.concatenate(next_parts, axis=1)
    return (next_first[None], next_grad[None])


def solution(mesh):
    in_specs = (
        P("pipe", "expert", None),
        P("pipe", "expert", None),
        P("pipe", "expert", None),
        P("pipe", "expert", None),
        P("pipe", "expert", None),
        P("pipe", "expert", None),
        P("pipe", "expert", None),
        P("pipe", None),
        P("pipe", None, "expert"),
        P("pipe", "expert", None),
        P("pipe", None),
        P("pipe", None, "expert"),
        P("pipe", "expert", None),
    )
    out_specs = (P("pipe", "expert", None), P("pipe", "expert", None))
    return jax.shard_map(
        per_device, mesh=mesh, in_specs=in_specs, out_specs=out_specs, check_vma=False
    )
```

```python
import functools

import jax
import jax.numpy as jnp
from jax import lax
from jax.experimental import pallas as pl
from jax.experimental.pallas import tpu as pltpu
from jax.sharding import PartitionSpec as P

SPLIT = 4
VMEM_LIMIT = 40 * 1024 * 1024
PREPARE_LIMIT = 60 * 1024 * 1024
PARAMS = pltpu.CompilerParams(vmem_limit_bytes=VMEM_LIMIT)
WHOLE = pl.BlockSpec(memory_space=pltpu.VMEM)


def shifted(block, axis, distance):
    devices = range(lax.axis_size(axis))
    route = [((i - distance) % len(devices), i) for i in devices]
    return lax.ppermute(block, axis, route)


def swapped(block, bit):
    return lax.ppermute(block, "expert", [(i, i ^ bit) for i in range(lax.axis_size("expert"))])


def after(block, *others):
    return lax.optimization_barrier((block, *others))[0]


def to_group(block, distance):
    owners = lax.axis_size("expert")
    return lax.ppermute(
        block, "expert", [(i, (i + distance * SPLIT) % owners) for i in range(owners)]
    )


def width_step(width):
    lanes = width // 128
    return 128 * max(n for n in range(1, 9) if lanes % n == 0)


def dot(left, right, left_dim, right_dim):
    return lax.dot_general(
        left, right, (((left_dim,), (right_dim,)), ((), ())), preferred_element_type=jnp.float32
    )


def as_column(row):
    tokens = row.shape[1]
    diagonal = lax.broadcasted_iota(jnp.int32, (tokens, tokens), 0) == lax.broadcasted_iota(
        jnp.int32, (tokens, tokens), 1
    )
    return jnp.sum(jnp.where(diagonal, row, 0.0), axis=1, keepdims=True)


def relative_groups(route_ref, groups):
    group = lax.axis_index("expert") // SPLIT
    ahead = as_column(route_ref[...].astype(jnp.float32)).astype(jnp.int32) - group
    return jnp.where(ahead < 0, ahead + groups, ahead)


def slot_numbers(relative):
    tokens = relative.shape[0]
    chosen = relative == lax.broadcasted_iota(jnp.int32, (tokens, 128), 1)
    onehot = jnp.where(chosen, 1.0, 0.0)
    earlier = lax.broadcasted_iota(jnp.int32, (tokens, tokens), 1) < lax.broadcasted_iota(
        jnp.int32, (tokens, tokens), 0
    )
    before = dot(
        jnp.where(earlier, 1.0, 0.0).astype(jnp.bfloat16), onehot.astype(jnp.bfloat16), 1, 0
    )
    return jnp.sum(before * onehot, axis=1, keepdims=True).astype(jnp.int32)


def placement(relative, slots, group, capacity):
    tokens = relative.shape[0]
    columns = lax.broadcasted_iota(jnp.int32, (tokens, capacity), 1)
    inside = jnp.where(relative == group, slots, -1)
    return jnp.where(inside == columns, 1.0, 0.0).astype(jnp.bfloat16)


def inverse_rms_of(acts_ref, step):
    width = acts_ref.shape[1]
    squares = 0.0
    for start in range(0, width, step):
        values = acts_ref[:, start : start + step].astype(jnp.float32)
        squares = squares + jnp.sum(values * values, axis=1, keepdims=True)
    return lax.rsqrt(squares / width + 1e-06)


def prepare_body(
    groups,
    capacity,
    step,
    route_first_ref,
    route_second_ref,
    weight_ref,
    acts_first_hbm,
    gain_first_hbm,
    acts_second_hbm,
    gain_second_hbm,
    grad_hbm,
    stay_first_ref,
    stay_second_ref,
    cross_first_ref,
    cross_second_ref,
    acts_first_ref,
    gain_first_ref,
    acts_second_ref,
    gain_second_ref,
    grad_ref,
    sems,
):
    sources = (acts_second_hbm, gain_second_hbm, grad_hbm, acts_first_hbm, gain_first_hbm)
    targets = (acts_second_ref, gain_second_ref, grad_ref, acts_first_ref, gain_first_ref)
    copies = [
        pltpu.make_async_copy(source, target, sems.at[n])
        for n, (source, target) in enumerate(zip(sources, targets))
    ]
    for copy in copies:
        copy.start()
    weight = as_column(weight_ref[...])
    places = []
    for route_ref in (route_first_ref, route_second_ref):
        relative = relative_groups(route_ref, groups)
        slots = slot_numbers(relative)
        places.append([placement(relative, slots, k, capacity) for k in range(groups)])

    def place(batch, row, stay_ref, cross_ref, value, part):
        stay_ref[row, :, part] = dot(places[batch][0], value, 0, 0).astype(jnp.bfloat16)
        for k in range(1, groups):
            there = dot(places[batch][k], value, 0, 0).astype(jnp.bfloat16)
            cross_ref[k - 1, row, :, part] = there

    parts = [
        slice(start, start + step) for start in range(0, acts_first_ref.shape[1], step)
    ]
    for copy in copies[:2]:
        copy.wait()
    inverse_rms = inverse_rms_of(acts_second_ref, step)
    for part in parts:
        normed = acts_second_ref[:, part].astype(jnp.float32) * inverse_rms * gain_second_ref[:, part]
        place(1, 0, stay_second_ref, cross_second_ref, normed.astype(jnp.bfloat16), part)
    copies[2].wait()
    for part in parts:
        scaled = weight * grad_ref[:, part].astype(jnp.float32)
        place(1, 1, stay_second_ref, cross_second_ref, scaled.astype(jnp.bfloat16), part)
    for copy in copies[3:]:
        copy.wait()
    inverse_rms = inverse_rms_of(acts_first_ref, step)
    for part in parts:
        normed = acts_first_ref[:, part].astype(jnp.float32) * inverse_rms * gain_first_ref[:, part]
        place(0, 0, stay_first_ref, cross_first_ref, normed.astype(jnp.bfloat16), part)


def prepare(groups, capacity, step, route_first, route_second, weight, *large):
    width = large[0].shape[1]
    shape = jax.ShapeDtypeStruct
    return pl.pallas_call(
        functools.partial(prepare_body, groups, capacity, step),
        in_specs=[WHOLE] * 3 + [pl.BlockSpec(memory_space=pl.ANY)] * 5,
        out_specs=[WHOLE] * 4,
        out_shape=[
            shape((1, capacity, width), jnp.bfloat16),
            shape((2, capacity, width), jnp.bfloat16),
            shape((groups - 1, 1, capacity, width), jnp.bfloat16),
            shape((groups - 1, 2, capacity, width), jnp.bfloat16),
        ],
        scratch_shapes=[pltpu.VMEM(array.shape, array.dtype) for array in large]
        + [pltpu.SemaphoreType.DMA((5,))],
        compiler_params=pltpu.CompilerParams(vmem_limit_bytes=PREPARE_LIMIT),
    )(route_first, route_second, weight, *large)


def backward_hidden_body(pieces, *refs):
    rows_refs = refs[:pieces]
    up_refs, down_refs = refs[pieces : pieces + 2], refs[pieces + 2 : pieces + 4]
    back_ref, upper_total, hidden_total = refs[pieces + 4 :]
    step, steps = pl.program_id(0), pl.num_programs(0)
    normed = jnp.concatenate([ref[0] for ref in rows_refs], axis=0)
    scaled = jnp.concatenate([ref[1] for ref in rows_refs], axis=0)
    hidden = up_refs[0].shape[1]

    @pl.when(step == 0)
    def _():
        upper_total[...] = jnp.zeros_like(upper_total)
        hidden_total[...] = jnp.zeros_like(hidden_total)

    for lane in range(2):
        part = slice(lane * hidden, (lane + 1) * hidden)
        upper_total[:, part] += dot(normed, up_refs[lane][...], 1, 0)
        hidden_total[:, part] += dot(scaled, down_refs[lane][...], 1, 1)

    @pl.when(step == steps - 1)
    def _():
        upper = upper_total[...]
        sigmoid = jax.nn.sigmoid(upper)
        back = hidden_total[...] * sigmoid * (1.0 + upper * (1.0 - sigmoid))
        back_ref[...] = back.astype(jnp.bfloat16)


def forward_hidden_body(pieces, *refs):
    rows_refs = refs[:pieces]
    up_refs = refs[pieces : pieces + 2]
    hidden_ref, upper_total = refs[pieces + 2 :]
    step, steps = pl.program_id(0), pl.num_programs(0)
    normed = jnp.concatenate([ref[0] for ref in rows_refs], axis=0)
    hidden = up_refs[0].shape[1]

    @pl.when(step == 0)
    def _():
        upper_total[...] = jnp.zeros_like(upper_total)

    for lane in range(2):
        part = slice(lane * hidden, (lane + 1) * hidden)
        upper_total[:, part] += dot(normed, up_refs[lane][...], 1, 0)

    @pl.when(step == steps - 1)
    def _():
        upper = upper_total[...]
        hidden_ref[...] = (upper * jax.nn.sigmoid(upper)).astype(jnp.bfloat16)


def spread_body(weights_dim, own_rows, hidden_ref, one_ref, other_ref, own_ref, away_ref):
    hidden = hidden_ref.shape[1] // 2
    contract = 1 if weights_dim == 0 else 0
    total = dot(hidden_ref[:, :hidden], one_ref[...], 1, contract)
    total = total + dot(hidden_ref[:, hidden:], other_ref[...], 1, contract)
    own_ref[...] = total[:own_rows]
    away_ref[...] = total[own_rows:].astype(jnp.bfloat16)


def spread(hidden_rows, one, other, weights_dim, first, length, step):
    own_rows = hidden_rows.shape[0] // 2
    offset = first // step
    if weights_dim == 0:
        block, index = (step, one.shape[1]), lambda j: (j + offset, 0)
    else:
        block, index = (one.shape[0], step), lambda j: (0, j + offset)
    return pl.pallas_call(
        functools.partial(spread_body, weights_dim, own_rows),
        grid=(length // step,),
        in_specs=[
            pl.BlockSpec(hidden_rows.shape, lambda j: (0, 0)),
            pl.BlockSpec(block, index),
            pl.BlockSpec(block, index),
        ],
        out_specs=[pl.BlockSpec((own_rows, step), lambda j: (0, j))] * 2,
        out_shape=[
            jax.ShapeDtypeStruct((own_rows, length), jnp.float32),
            jax.ShapeDtypeStruct((own_rows, length), jnp.bfloat16),
        ],
        compiler_params=PARAMS,
    )(hidden_rows, one, other)


def collected(relative, groups, capacity, own, partner, returned):
    slots = slot_numbers(relative)
    stay = own + partner.astype(jnp.float32)
    high = stay.astype(jnp.bfloat16)
    low = (stay - high.astype(jnp.float32)).astype(jnp.bfloat16)
    here = placement(relative, slots, 0, capacity)
    total = dot(here, high, 1, 0) + dot(here, low, 1, 0)
    away = (groups - 1) * capacity
    columns = lax.broadcasted_iota(jnp.int32, (relative.shape[0], away), 1)
    inside = jnp.where(relative > 0, (relative - 1) * capacity + slots, -1)
    there = jnp.where(inside == columns, 1.0, 0.0).astype(jnp.bfloat16)
    return total + dot(there, returned, 1, 0)


def finish_first_body(
    groups, capacity, route_ref, weight_ref, acts_ref, own_ref, partner_ref, returned_ref, out_ref
):
    relative = relative_groups(route_ref, groups)
    total = collected(relative, groups, capacity, own_ref[...], partner_ref[...], returned_ref[...])
    weight = as_column(weight_ref[...])
    out_ref[...] = (acts_ref[...].astype(jnp.float32) + weight * total).astype(jnp.bfloat16)


def finish_second_body(
    groups,
    capacity,
    step,
    route_ref,
    acts_ref,
    grad_ref,
    gain_ref,
    own_ref,
    partner_ref,
    returned_ref,
    out_ref,
    gained,
):
    width = acts_ref.shape[1]
    relative = relative_groups(route_ref, groups)
    inverse_rms = inverse_rms_of(acts_ref, step)
    along = 0.0
    for start in range(0, width, step):
        part = slice(start, start + step)
        total = collected(
            relative, groups, capacity, own_ref[:, part], partner_ref[:, part], returned_ref[:, part]
        )
        total = gain_ref[:, part] * total
        gained[:, part] = total
        along = along + jnp.sum(
            acts_ref[:, part].astype(jnp.float32) * total, axis=1, keepdims=True
        )
    scale = inverse_rms * inverse_rms * inverse_rms * (along / width)
    for start in range(0, width, step):
        part = slice(start, start + step)
        values = acts_ref[:, part].astype(jnp.float32)
        out = grad_ref[:, part].astype(jnp.float32) + inverse_rms * gained[:, part] - values * scale
        out_ref[:, part] = out.astype(jnp.bfloat16)


def columns_block(length, number, rows):
    return pl.BlockSpec((rows, length), lambda j: (0, number))


def rows_blocks(arrays, step):
    specs = []
    for array in arrays:
        lead = array.shape[:-1]
        specs.append(pl.BlockSpec((*lead, step), lambda j, zeros=(0,) * len(lead): (*zeros, j)))
    return specs


def per_device(
    acts_first,
    route_first,
    weight_first,
    acts_second,
    grad_second,
    route_second,
    weight_second,
    gain_first,
    up_first,
    down_first,
    gain_second,
    up_second,
    down_second,
):
    owners = lax.axis_size("expert")
    groups = owners // SPLIT
    tokens, width = acts_first.shape[1:]
    capacity = 3 * tokens * SPLIT // (2 * owners)
    away = (groups - 1) * capacity
    step = width_step(width)
    hidden = up_first.shape[2]
    bf16 = jnp.bfloat16
    routes = [route.reshape(1, tokens) for route in (route_first, route_second)]
    weights = [weight.reshape(1, tokens) for weight in (weight_first, weight_second)]
    parts = 2 if (width // step) % 2 == 0 else 1
    length = width // parts
    starts = range(0, width, length)

    down_second_other = swapped(down_second[0], 2)
    up_first_other = swapped(up_first[0], 1)
    stay_first, stay_second, cross_first, cross_second = prepare(
        groups,
        capacity,
        step,
        *routes,
        weights[1],
        acts_first[0],
        gain_first,
        acts_second[0],
        gain_second,
        grad_second[0],
    )

    def crossed(blocks):
        came = [to_group(blocks[k - 1], k) for k in range(1, groups)]
        return came[0] if groups == 2 else jnp.concatenate(came, axis=1)

    came_second = crossed(cross_second)
    stay_second_other = swapped(after(stay_second, up_first_other), 1)
    up_second_other = swapped(after(up_second[0], up_first_other), 2)
    came_first = crossed(after(cross_first, up_second_other))
    down_first_other = swapped(after(down_first[0], up_first_other), 1)
    came_second = after(came_second, down_second_other, stay_second_other)
    came_second_other = swapped(came_second, 1)
    stay_first_other = swapped(after(stay_first, up_second_other), 2)
    came_first_other = swapped(came_first, 2)

    rows = [stay_second, came_second, stay_second_other, came_second_other]
    if capacity % 16:
        rows = [jnp.concatenate(rows, axis=1)]
    both = 2 * (capacity + away)
    back_upper = pl.pallas_call(
        functools.partial(backward_hidden_body, len(rows)),
        grid=(width // step,),
        in_specs=rows_blocks(rows, step)
        + [pl.BlockSpec((step, hidden), lambda j: (j, 0))] * 2
        + [pl.BlockSpec((hidden, step), lambda j: (0, j))] * 2,
        out_specs=pl.BlockSpec((both, 2 * hidden), lambda j: (0, 0)),
        out_shape=jax.ShapeDtypeStruct((both, 2 * hidden), bf16),
        scratch_shapes=[pltpu.VMEM((both, 2 * hidden), jnp.float32)] * 2,
        compiler_params=PARAMS,
    )(*rows, up_second[0], up_second_other, down_second[0], down_second_other)
    own_second, send_second = spread(
        back_upper, up_second[0], up_second_other, 0, 0, width, step
    )
    came_part = swapped(send_second[capacity:], 1)
    stay_part = swapped(send_second[:capacity], 1)
    def first_hidden(rows):
        if capacity % 16:
            rows = [jnp.concatenate(rows, axis=1)]
        count = sum(array.shape[1] for array in rows)
        return pl.pallas_call(
            functools.partial(forward_hidden_body, len(rows)),
            grid=(width // step,),
            in_specs=rows_blocks(rows, step) + [pl.BlockSpec((step, hidden), lambda j: (j, 0))] * 2,
            out_specs=pl.BlockSpec((count, 2 * hidden), lambda j: (0, 0)),
            out_shape=jax.ShapeDtypeStruct((count, 2 * hidden), bf16),
            scratch_shapes=[pltpu.VMEM((count, 2 * hidden), jnp.float32)],
            compiler_params=PARAMS,
        )(*rows, up_first[0], up_first_other)

    weights_down = (down_first[0], down_first_other, 1)
    stay_hidden = first_hidden([after(stay_first, send_second), stay_first_other])
    stay_own, stay_send = spread(stay_hidden, *weights_down, 0, width, step)
    stay_first_part = swapped(stay_send, 2)
    back = (own_second[capacity:] + after(came_part, stay_send).astype(jnp.float32)).astype(bf16)
    returned = [
        to_group(back[(k - 1) * capacity : k * capacity], groups - k) for k in range(1, groups)
    ]
    returned = returned[0] if groups == 2 else jnp.concatenate(returned, axis=0)
    came_hidden = first_hidden([came_first, after(came_first_other, stay_send)])
    spreads = [spread(came_hidden, *weights_down, first, length, step) for first in starts]
    came_parts = [swapped(send, 2) for _, send in spreads]
    returned_first = []
    for (own, _), part in zip(spreads, came_parts):
        back = (own + part.astype(jnp.float32)).astype(bf16)
        blocks = [
            to_group(back[(k - 1) * capacity : k * capacity], groups - k)
            for k in range(1, groups)
        ]
        returned_first.append(blocks[0] if groups == 2 else jnp.concatenate(blocks, axis=0))

    grad_acts = pl.pallas_call(
        functools.partial(finish_second_body, groups, capacity, step),
        in_specs=[WHOLE] * 7,
        out_specs=WHOLE,
        out_shape=jax.ShapeDtypeStruct((tokens, width), bf16),
        scratch_shapes=[pltpu.VMEM((tokens, width), jnp.float32)],
        compiler_params=PARAMS,
    )(
        routes[1],
        acts_second[0],
        grad_second[0],
        gain_second,
        own_second[:capacity],
        stay_part,
        returned,
    )
    next_grad = shifted(grad_acts, "pipe", 1)
    next_parts = []
    order = [grad_acts, next_grad]
    for first, back in zip(starts, returned_first):
        half = functools.partial(columns_block, length, first // length)
        mixed = pl.pallas_call(
            functools.partial(finish_first_body, groups, capacity),
            grid=(1,),
            in_specs=[WHOLE] * 2 + [half(tokens), half(capacity), half(capacity), WHOLE],
            out_specs=WHOLE,
            out_shape=jax.ShapeDtypeStruct((tokens, length), bf16),
            compiler_params=PARAMS,
        )(
            routes[0],
            weights[0],
            after(acts_first[0], order[first > 0]),
            stay_own,
            stay_first_part,
            back,
        )
        next_parts.append(shifted(mixed, "pipe", 1))
    next_first = next_parts[0] if parts == 1 else jnp.concatenate(next_parts, axis=1)
    return (next_first[None], next_grad[None])


def solution(mesh):
    in_specs = (
        P("pipe", "expert", None),
        P("pipe", "expert", None),
        P("pipe", "expert", None),
        P("pipe", "expert", None),
        P("pipe", "expert", None),
        P("pipe", "expert", None),
        P("pipe", "expert", None),
        P("pipe", None),
        P("pipe", None, "expert"),
        P("pipe", "expert", None),
        P("pipe", None),
        P("pipe", None, "expert"),
        P("pipe", "expert", None),
    )
    out_specs = (P("pipe", "expert", None), P("pipe", "expert", None))
    return jax.shard_map(
        per_device, mesh=mesh, in_specs=in_specs, out_specs=out_specs, check_vma=False
    )
```

```python
import functools

import jax
import jax.numpy as jnp
from jax import lax
from jax.experimental import pallas as pl
from jax.experimental.pallas import tpu as pltpu
from jax.sharding import PartitionSpec as P

SPLIT = 4
VMEM_LIMIT = 40 * 1024 * 1024
PREPARE_LIMIT = 60 * 1024 * 1024
PARAMS = pltpu.CompilerParams(vmem_limit_bytes=VMEM_LIMIT)
WHOLE = pl.BlockSpec(memory_space=pltpu.VMEM)


def to_group_ahead(block, distance):
    owners, stages = lax.axis_size("expert"), lax.axis_size("pipe")
    route = [
        (p * owners + i, (p + 1) % stages * owners + (i + distance * SPLIT) % owners)
        for p in range(stages)
        for i in range(owners)
    ]
    return lax.ppermute(block, ("pipe", "expert"), route)


def shifted(block, axis, distance):
    devices = range(lax.axis_size(axis))
    route = [((i - distance) % len(devices), i) for i in devices]
    return lax.ppermute(block, axis, route)


def swapped(block, bit):
    return lax.ppermute(block, "expert", [(i, i ^ bit) for i in range(lax.axis_size("expert"))])


def after(block, *others):
    return lax.optimization_barrier((block, *others))[0]


def to_group(block, distance):
    owners = lax.axis_size("expert")
    return lax.ppermute(
        block, "expert", [(i, (i + distance * SPLIT) % owners) for i in range(owners)]
    )


def width_step(width):
    lanes = width // 128
    return 128 * max(n for n in range(1, 9) if lanes % n == 0)


def dot(left, right, left_dim, right_dim):
    return lax.dot_general(
        left, right, (((left_dim,), (right_dim,)), ((), ())), preferred_element_type=jnp.float32
    )


def as_column(row):
    tokens = row.shape[1]
    diagonal = lax.broadcasted_iota(jnp.int32, (tokens, tokens), 0) == lax.broadcasted_iota(
        jnp.int32, (tokens, tokens), 1
    )
    return jnp.sum(jnp.where(diagonal, row, 0.0), axis=1, keepdims=True)


def relative_groups(route_ref, groups):
    group = lax.axis_index("expert") // SPLIT
    ahead = as_column(route_ref[...].astype(jnp.float32)).astype(jnp.int32) - group
    return jnp.where(ahead < 0, ahead + groups, ahead)


def slot_numbers(relative):
    tokens = relative.shape[0]
    chosen = relative == lax.broadcasted_iota(jnp.int32, (tokens, 128), 1)
    onehot = jnp.where(chosen, 1.0, 0.0)
    earlier = lax.broadcasted_iota(jnp.int32, (tokens, tokens), 1) < lax.broadcasted_iota(
        jnp.int32, (tokens, tokens), 0
    )
    before = dot(
        jnp.where(earlier, 1.0, 0.0).astype(jnp.bfloat16), onehot.astype(jnp.bfloat16), 1, 0
    )
    return jnp.sum(before * onehot, axis=1, keepdims=True).astype(jnp.int32)


def placement(relative, slots, group, capacity):
    tokens = relative.shape[0]
    columns = lax.broadcasted_iota(jnp.int32, (tokens, capacity), 1)
    inside = jnp.where(relative == group, slots, -1)
    return jnp.where(inside == columns, 1.0, 0.0).astype(jnp.bfloat16)


def inverse_rms_of(acts_ref, step):
    width = acts_ref.shape[1]
    squares = 0.0
    for start in range(0, width, step):
        values = acts_ref[:, start : start + step].astype(jnp.float32)
        squares = squares + jnp.sum(values * values, axis=1, keepdims=True)
    return lax.rsqrt(squares / width + 1e-06)


def prepare_body(
    groups,
    capacity,
    step,
    route_first_ref,
    route_second_ref,
    weight_ref,
    acts_first_hbm,
    gain_first_hbm,
    acts_second_hbm,
    gain_second_hbm,
    grad_hbm,
    stay_first_ref,
    stay_second_ref,
    cross_first_ref,
    cross_second_ref,
    acts_first_ref,
    gain_first_ref,
    acts_second_ref,
    gain_second_ref,
    grad_ref,
    sems,
):
    sources = (acts_second_hbm, gain_second_hbm, grad_hbm, acts_first_hbm, gain_first_hbm)
    targets = (acts_second_ref, gain_second_ref, grad_ref, acts_first_ref, gain_first_ref)
    copies = [
        pltpu.make_async_copy(source, target, sems.at[n])
        for n, (source, target) in enumerate(zip(sources, targets))
    ]
    for copy in copies:
        copy.start()
    weight = as_column(weight_ref[...])
    places = []
    for route_ref in (route_first_ref, route_second_ref):
        relative = relative_groups(route_ref, groups)
        slots = slot_numbers(relative)
        places.append([placement(relative, slots, k, capacity) for k in range(groups)])

    def place(batch, row, stay_ref, cross_ref, value, part):
        stay_ref[row, :, part] = dot(places[batch][0], value, 0, 0).astype(jnp.bfloat16)
        for k in range(1, groups):
            there = dot(places[batch][k], value, 0, 0).astype(jnp.bfloat16)
            cross_ref[k - 1, row, :, part] = there

    parts = [
        slice(start, start + step) for start in range(0, acts_first_ref.shape[1], step)
    ]
    for copy in copies[:2]:
        copy.wait()
    inverse_rms = inverse_rms_of(acts_second_ref, step)
    for part in parts:
        normed = acts_second_ref[:, part].astype(jnp.float32) * inverse_rms * gain_second_ref[:, part]
        place(1, 0, stay_second_ref, cross_second_ref, normed.astype(jnp.bfloat16), part)
    copies[2].wait()
    for part in parts:
        scaled = weight * grad_ref[:, part].astype(jnp.float32)
        place(1, 1, stay_second_ref, cross_second_ref, scaled.astype(jnp.bfloat16), part)
    for copy in copies[3:]:
        copy.wait()
    inverse_rms = inverse_rms_of(acts_first_ref, step)
    for part in parts:
        normed = acts_first_ref[:, part].astype(jnp.float32) * inverse_rms * gain_first_ref[:, part]
        place(0, 0, stay_first_ref, cross_first_ref, normed.astype(jnp.bfloat16), part)


def prepare(groups, capacity, step, route_first, route_second, weight, *large):
    width = large[0].shape[1]
    shape = jax.ShapeDtypeStruct
    return pl.pallas_call(
        functools.partial(prepare_body, groups, capacity, step),
        in_specs=[WHOLE] * 3 + [pl.BlockSpec(memory_space=pl.ANY)] * 5,
        out_specs=[WHOLE] * 4,
        out_shape=[
            shape((1, capacity, width), jnp.bfloat16),
            shape((2, capacity, width), jnp.bfloat16),
            shape((groups - 1, 1, capacity, width), jnp.bfloat16),
            shape((groups - 1, 2, capacity, width), jnp.bfloat16),
        ],
        scratch_shapes=[pltpu.VMEM(array.shape, array.dtype) for array in large]
        + [pltpu.SemaphoreType.DMA((5,))],
        compiler_params=pltpu.CompilerParams(vmem_limit_bytes=PREPARE_LIMIT),
    )(route_first, route_second, weight, *large)


def backward_hidden_body(pieces, *refs):
    rows_refs = refs[:pieces]
    up_refs, down_refs = refs[pieces : pieces + 2], refs[pieces + 2 : pieces + 4]
    back_ref, upper_total, hidden_total = refs[pieces + 4 :]
    step, steps = pl.program_id(0), pl.num_programs(0)
    normed = jnp.concatenate([ref[0] for ref in rows_refs], axis=0)
    scaled = jnp.concatenate([ref[1] for ref in rows_refs], axis=0)
    hidden = up_refs[0].shape[1]

    @pl.when(step == 0)
    def _():
        upper_total[...] = jnp.zeros_like(upper_total)
        hidden_total[...] = jnp.zeros_like(hidden_total)

    for lane in range(2):
        part = slice(lane * hidden, (lane + 1) * hidden)
        upper_total[:, part] += dot(normed, up_refs[lane][...], 1, 0)
        hidden_total[:, part] += dot(scaled, down_refs[lane][...], 1, 1)

    @pl.when(step == steps - 1)
    def _():
        upper = upper_total[...]
        sigmoid = jax.nn.sigmoid(upper)
        back = hidden_total[...] * sigmoid * (1.0 + upper * (1.0 - sigmoid))
        back_ref[...] = back.astype(jnp.bfloat16)


def forward_hidden_body(pieces, *refs):
    rows_refs = refs[:pieces]
    up_refs = refs[pieces : pieces + 2]
    hidden_ref, upper_total = refs[pieces + 2 :]
    step, steps = pl.program_id(0), pl.num_programs(0)
    normed = jnp.concatenate([ref[0] for ref in rows_refs], axis=0)
    hidden = up_refs[0].shape[1]

    @pl.when(step == 0)
    def _():
        upper_total[...] = jnp.zeros_like(upper_total)

    for lane in range(2):
        part = slice(lane * hidden, (lane + 1) * hidden)
        upper_total[:, part] += dot(normed, up_refs[lane][...], 1, 0)

    @pl.when(step == steps - 1)
    def _():
        upper = upper_total[...]
        hidden_ref[...] = (upper * jax.nn.sigmoid(upper)).astype(jnp.bfloat16)


def spread_body(weights_dim, own_rows, hidden_ref, one_ref, other_ref, own_ref, away_ref):
    hidden = hidden_ref.shape[1] // 2
    contract = 1 if weights_dim == 0 else 0
    total = dot(hidden_ref[:, :hidden], one_ref[...], 1, contract)
    total = total + dot(hidden_ref[:, hidden:], other_ref[...], 1, contract)
    own_ref[...] = total[:own_rows]
    away_ref[...] = total[own_rows:].astype(jnp.bfloat16)


def spread(hidden_rows, one, other, weights_dim, first, length, step):
    own_rows = hidden_rows.shape[0] // 2
    offset = first // step
    if weights_dim == 0:
        block, index = (step, one.shape[1]), lambda j: (j + offset, 0)
    else:
        block, index = (one.shape[0], step), lambda j: (0, j + offset)
    return pl.pallas_call(
        functools.partial(spread_body, weights_dim, own_rows),
        grid=(length // step,),
        in_specs=[
            pl.BlockSpec(hidden_rows.shape, lambda j: (0, 0)),
            pl.BlockSpec(block, index),
            pl.BlockSpec(block, index),
        ],
        out_specs=[pl.BlockSpec((own_rows, step), lambda j: (0, j))] * 2,
        out_shape=[
            jax.ShapeDtypeStruct((own_rows, length), jnp.float32),
            jax.ShapeDtypeStruct((own_rows, length), jnp.bfloat16),
        ],
        compiler_params=PARAMS,
    )(hidden_rows, one, other)


def away_placement(relative, groups, capacity):
    away = (groups - 1) * capacity
    columns = lax.broadcasted_iota(jnp.int32, (relative.shape[0], away), 1)
    inside = jnp.where(relative > 0, (relative - 1) * capacity + slot_numbers(relative), -1)
    return jnp.where(inside == columns, 1.0, 0.0).astype(jnp.bfloat16)


def collected(relative, groups, capacity, own, partner, returned):
    slots = slot_numbers(relative)
    stay = own + partner.astype(jnp.float32)
    high = stay.astype(jnp.bfloat16)
    low = (stay - high.astype(jnp.float32)).astype(jnp.bfloat16)
    here = placement(relative, slots, 0, capacity)
    total = dot(here, high, 1, 0) + dot(here, low, 1, 0)
    return total + dot(away_placement(relative, groups, capacity), returned, 1, 0)


def finish_stay_body(
    groups, capacity, step, route_ref, weight_ref, acts_ref, own_ref, partner_ref, *out_refs
):
    relative = relative_groups(route_ref, groups)
    here = placement(relative, slot_numbers(relative), 0, capacity)
    weight = as_column(weight_ref[...])
    for start in range(0, acts_ref.shape[1], step):
        part = slice(start, start + step)
        stay = own_ref[:, part] + partner_ref[:, part].astype(jnp.float32)
        high = stay.astype(jnp.bfloat16)
        low = (stay - high.astype(jnp.float32)).astype(jnp.bfloat16)
        total = dot(here, high, 1, 0) + dot(here, low, 1, 0)
        out = acts_ref[:, part].astype(jnp.float32) + weight * total
        length = out_refs[0].shape[1]
        first = start % length
        out_refs[start // length][:, first : first + step] = out.astype(jnp.bfloat16)


def finish_came_body(groups, capacity, part, pieces, notes_ref, returned_ref, *refs):
    out_hbm, out_ref, sem = refs[-3:]
    relative = relative_groups(notes_ref.at[0:1], groups)
    there = away_placement(relative, groups, capacity)
    weight = as_column(notes_ref[1:2])
    width = out_ref.shape[1] // pieces
    for n, stayed_ref in enumerate(refs[:pieces]):
        piece = slice(n * width, (n + 1) * width)
        total = dot(there, returned_ref[:, piece], 1, 0)
        out = stayed_ref[...].astype(jnp.float32) + weight * total
        out_ref[:, piece] = out.astype(jnp.bfloat16)
    copy = pltpu.make_async_copy(out_ref, out_hbm.at[:, part], sem)
    copy.start()
    copy.wait()


def finish_second_body(
    groups,
    capacity,
    step,
    route_ref,
    acts_ref,
    grad_ref,
    gain_ref,
    own_ref,
    partner_ref,
    returned_ref,
    out_ref,
    gained,
):
    width = acts_ref.shape[1]
    relative = relative_groups(route_ref, groups)
    inverse_rms = inverse_rms_of(acts_ref, step)
    along = 0.0
    for start in range(0, width, step):
        part = slice(start, start + step)
        total = collected(
            relative, groups, capacity, own_ref[:, part], partner_ref[:, part], returned_ref[:, part]
        )
        total = gain_ref[:, part] * total
        gained[:, part] = total
        along = along + jnp.sum(
            acts_ref[:, part].astype(jnp.float32) * total, axis=1, keepdims=True
        )
    scale = inverse_rms * inverse_rms * inverse_rms * (along / width)
    for start in range(0, width, step):
        part = slice(start, start + step)
        values = acts_ref[:, part].astype(jnp.float32)
        out = grad_ref[:, part].astype(jnp.float32) + inverse_rms * gained[:, part] - values * scale
        out_ref[:, part] = out.astype(jnp.bfloat16)


def rows_blocks(arrays, step):
    specs = []
    for array in arrays:
        lead = array.shape[:-1]
        specs.append(pl.BlockSpec((*lead, step), lambda j, zeros=(0,) * len(lead): (*zeros, j)))
    return specs


def per_device(
    acts_first,
    route_first,
    weight_first,
    acts_second,
    grad_second,
    route_second,
    weight_second,
    gain_first,
    up_first,
    down_first,
    gain_second,
    up_second,
    down_second,
):
    owners = lax.axis_size("expert")
    groups = owners // SPLIT
    tokens, width = acts_first.shape[1:]
    capacity = 3 * tokens * SPLIT // (2 * owners)
    away = (groups - 1) * capacity
    step = width_step(width)
    hidden = up_first.shape[2]
    bf16 = jnp.bfloat16
    routes = [route.reshape(1, tokens) for route in (route_first, route_second)]
    weights = [weight.reshape(1, tokens) for weight in (weight_first, weight_second)]
    halves = 2 if width // 128 % 2 == 0 else 1
    length = width // halves
    per_half = 2 if length // 128 % 2 == 0 else 1
    piece = length // per_half
    step = width_step(piece)
    parts = [slice(first, first + length) for first in range(0, width, length)]

    def crossed(blocks):
        came = [to_group(blocks[k - 1], k) for k in range(1, groups)]
        return came[0] if groups == 2 else jnp.concatenate(came, axis=1)

    def returned_rows(rows, send=to_group):
        blocks = [
            send(rows[(k - 1) * capacity : k * capacity], groups - k) for k in range(1, groups)
        ]
        return blocks[0] if groups == 2 else jnp.concatenate(blocks, axis=0)

    down_second_other = swapped(down_second[0], 2)
    up_first_other = swapped(up_first[0], 1)
    stay_first, stay_second, cross_first, cross_second = prepare(
        groups,
        capacity,
        step,
        *routes,
        weights[1],
        acts_first[0],
        gain_first,
        acts_second[0],
        gain_second,
        grad_second[0],
    )
    notes = jnp.concatenate([routes[0].astype(jnp.float32), weights[0]])
    notes = shifted(after(notes, up_first_other), "pipe", 1)
    came_second = crossed(cross_second)
    stay_second_other = swapped(after(stay_second, up_first_other), 1)
    up_second_other = swapped(after(up_second[0], up_first_other), 2)
    down_first_other = swapped(after(down_first[0], up_first_other), 1)
    came_second = after(came_second, down_second_other, stay_second_other, notes)
    came_second_other = swapped(came_second, 1)
    came_first = crossed(after(cross_first, up_second_other))
    stay_first_other = swapped(after(stay_first, up_second_other), 2)

    rows = [stay_second, came_second, stay_second_other, came_second_other]
    if capacity % 16:
        rows = [jnp.concatenate(rows, axis=1)]
    both = 2 * (capacity + away)
    back_upper = pl.pallas_call(
        functools.partial(backward_hidden_body, len(rows)),
        grid=(width // step,),
        in_specs=rows_blocks(rows, step)
        + [pl.BlockSpec((step, hidden), lambda j: (j, 0))] * 2
        + [pl.BlockSpec((hidden, step), lambda j: (0, j))] * 2,
        out_specs=pl.BlockSpec((both, 2 * hidden), lambda j: (0, 0)),
        out_shape=jax.ShapeDtypeStruct((both, 2 * hidden), bf16),
        scratch_shapes=[pltpu.VMEM((both, 2 * hidden), jnp.float32)] * 2,
        compiler_params=PARAMS,
    )(*rows, up_second[0], up_second_other, down_second[0], down_second_other)
    own_second, send_second = spread(back_upper, up_second[0], up_second_other, 0, 0, width, step)
    came_part = swapped(send_second[capacity:], 1)
    stay_part = swapped(after(send_second[:capacity], came_part), 1)

    came_first_other = swapped(came_first, 2)

    def first_hidden(rows):
        if capacity % 16:
            rows = [jnp.concatenate(rows, axis=1)]
        count = sum(array.shape[1] for array in rows)
        return pl.pallas_call(
            functools.partial(forward_hidden_body, len(rows)),
            grid=(width // step,),
            in_specs=rows_blocks(rows, step) + [pl.BlockSpec((step, hidden), lambda j: (j, 0))] * 2,
            out_specs=pl.BlockSpec((count, 2 * hidden), lambda j: (0, 0)),
            out_shape=jax.ShapeDtypeStruct((count, 2 * hidden), bf16),
            scratch_shapes=[pltpu.VMEM((count, 2 * hidden), jnp.float32)],
            compiler_params=PARAMS,
        )(*rows, up_first[0], up_first_other)

    weights_down = (down_first[0], down_first_other, 1)
    stay_hidden = first_hidden([after(stay_first, send_second), stay_first_other])
    stay_own, stay_send = spread(stay_hidden, *weights_down, 0, width, step)
    back = (own_second[capacity:] + after(came_part, stay_send).astype(jnp.float32)).astype(bf16)
    returned = returned_rows(back)
    came_hidden = first_hidden([came_first, came_first_other])
    spreads = [
        spread(came_hidden, *weights_down, part.start, length, step) for part in parts
    ]
    came_parts = [swapped(send, 2) for _, send in spreads]
    stay_first_part = swapped(after(stay_send, *came_parts), 2)
    backs = [
        (own + part.astype(jnp.float32)).astype(bf16) for (own, _), part in zip(spreads, came_parts)
    ]
    returned_first = [returned_rows(rows, to_group_ahead) for rows in backs]

    grad_acts = pl.pallas_call(
        functools.partial(finish_second_body, groups, capacity, step),
        in_specs=[WHOLE] * 7,
        out_specs=WHOLE,
        out_shape=jax.ShapeDtypeStruct((tokens, width), bf16),
        scratch_shapes=[pltpu.VMEM((tokens, width), jnp.float32)],
        compiler_params=PARAMS,
    )(
        routes[1],
        acts_second[0],
        grad_second[0],
        gain_second,
        own_second[:capacity],
        stay_part,
        returned,
    )
    next_grad = shifted(grad_acts, "pipe", 1)
    stayed = pl.pallas_call(
        functools.partial(finish_stay_body, groups, capacity, step),
        in_specs=[WHOLE] * 5,
        out_specs=[WHOLE] * (halves * per_half),
        out_shape=[jax.ShapeDtypeStruct((tokens, piece), bf16)] * (halves * per_half),
        compiler_params=PARAMS,
    )(routes[0], weights[0], after(acts_first[0], next_grad), stay_own, stay_first_part)
    stayed = [shifted(part, "pipe", 1) for part in stayed]

    next_first = []
    for n, (part, rows) in enumerate(zip(parts, returned_first)):
        pieces = stayed[n * per_half : (n + 1) * per_half]
        next_first = [
            pl.pallas_call(
                functools.partial(finish_came_body, groups, capacity, part, per_half),
                in_specs=[WHOLE] * (2 + per_half)
                + [pl.BlockSpec(memory_space=pl.ANY)] * len(next_first),
                out_specs=pl.BlockSpec(memory_space=pl.ANY),
                out_shape=jax.ShapeDtypeStruct((tokens, width), bf16),
                scratch_shapes=[pltpu.VMEM((tokens, length), bf16), pltpu.SemaphoreType.DMA],
                input_output_aliases={2 + per_half: 0} if next_first else {},
                compiler_params=PARAMS,
            )(notes, rows, *pieces, *next_first)
        ]
    return (next_first[0][None], next_grad[None])


def solution(mesh):
    in_specs = (
        P("pipe", "expert", None),
        P("pipe", "expert", None),
        P("pipe", "expert", None),
        P("pipe", "expert", None),
        P("pipe", "expert", None),
        P("pipe", "expert", None),
        P("pipe", "expert", None),
        P("pipe", None),
        P("pipe", None, "expert"),
        P("pipe", "expert", None),
        P("pipe", None),
        P("pipe", None, "expert"),
        P("pipe", "expert", None),
    )
    out_specs = (P("pipe", "expert", None), P("pipe", "expert", None))
    return jax.shard_map(
        per_device, mesh=mesh, in_specs=in_specs, out_specs=out_specs, check_vma=False
    )
```

```python
import functools

import jax
import jax.numpy as jnp
from jax import lax
from jax.experimental import pallas as pl
from jax.experimental.pallas import tpu as pltpu
from jax.sharding import PartitionSpec as P

SPLIT = 4
VMEM_LIMIT = 40 * 1024 * 1024
PREPARE_LIMIT = 60 * 1024 * 1024
PARAMS = pltpu.CompilerParams(vmem_limit_bytes=VMEM_LIMIT)
WHOLE = pl.BlockSpec(memory_space=pltpu.VMEM)


def to_group_ahead(block, distance):
    owners, stages = lax.axis_size("expert"), lax.axis_size("pipe")
    route = [
        (p * owners + i, (p + 1) % stages * owners + (i + distance * SPLIT) % owners)
        for p in range(stages)
        for i in range(owners)
    ]
    return lax.ppermute(block, ("pipe", "expert"), route)


def shifted(block, axis, distance):
    devices = range(lax.axis_size(axis))
    route = [((i - distance) % len(devices), i) for i in devices]
    return lax.ppermute(block, axis, route)


def swapped(block, bit):
    return lax.ppermute(block, "expert", [(i, i ^ bit) for i in range(lax.axis_size("expert"))])


def after(block, *others):
    return lax.optimization_barrier((block, *others))[0]


def to_group(block, distance):
    owners = lax.axis_size("expert")
    return lax.ppermute(
        block, "expert", [(i, (i + distance * SPLIT) % owners) for i in range(owners)]
    )


def width_step(width):
    lanes = width // 128
    return 128 * max(n for n in range(1, 9) if lanes % n == 0)


def dot(left, right, left_dim, right_dim):
    return lax.dot_general(
        left, right, (((left_dim,), (right_dim,)), ((), ())), preferred_element_type=jnp.float32
    )


def as_column(row):
    tokens = row.shape[1]
    diagonal = lax.broadcasted_iota(jnp.int32, (tokens, tokens), 0) == lax.broadcasted_iota(
        jnp.int32, (tokens, tokens), 1
    )
    return jnp.sum(jnp.where(diagonal, row, 0.0), axis=1, keepdims=True)


def relative_groups(route_ref, groups):
    group = lax.axis_index("expert") // SPLIT
    ahead = as_column(route_ref[...].astype(jnp.float32)).astype(jnp.int32) - group
    return jnp.where(ahead < 0, ahead + groups, ahead)


def slot_numbers(relative):
    tokens = relative.shape[0]
    chosen = relative == lax.broadcasted_iota(jnp.int32, (tokens, 128), 1)
    onehot = jnp.where(chosen, 1.0, 0.0)
    earlier = lax.broadcasted_iota(jnp.int32, (tokens, tokens), 1) < lax.broadcasted_iota(
        jnp.int32, (tokens, tokens), 0
    )
    before = dot(
        jnp.where(earlier, 1.0, 0.0).astype(jnp.bfloat16), onehot.astype(jnp.bfloat16), 1, 0
    )
    return jnp.sum(before * onehot, axis=1, keepdims=True).astype(jnp.int32)


def placement(relative, slots, group, capacity):
    tokens = relative.shape[0]
    columns = lax.broadcasted_iota(jnp.int32, (tokens, capacity), 1)
    inside = jnp.where(relative == group, slots, -1)
    return jnp.where(inside == columns, 1.0, 0.0).astype(jnp.bfloat16)


def inverse_rms_of(acts_ref, step):
    width = acts_ref.shape[1]
    squares = 0.0
    for start in range(0, width, step):
        values = acts_ref[:, start : start + step].astype(jnp.float32)
        squares = squares + jnp.sum(values * values, axis=1, keepdims=True)
    return lax.rsqrt(squares / width + 1e-06)


def prepare_body(
    groups,
    capacity,
    step,
    route_first_ref,
    route_second_ref,
    weight_ref,
    acts_first_hbm,
    gain_first_hbm,
    acts_second_hbm,
    gain_second_hbm,
    grad_hbm,
    stay_first_ref,
    stay_second_ref,
    cross_first_ref,
    cross_second_ref,
    acts_first_ref,
    gain_first_ref,
    acts_second_ref,
    gain_second_ref,
    grad_ref,
    sems,
):
    sources = (acts_second_hbm, gain_second_hbm, grad_hbm, acts_first_hbm, gain_first_hbm)
    targets = (acts_second_ref, gain_second_ref, grad_ref, acts_first_ref, gain_first_ref)
    copies = [
        pltpu.make_async_copy(source, target, sems.at[n])
        for n, (source, target) in enumerate(zip(sources, targets))
    ]
    for copy in copies:
        copy.start()
    weight = as_column(weight_ref[...])
    places = []
    for route_ref in (route_first_ref, route_second_ref):
        relative = relative_groups(route_ref, groups)
        slots = slot_numbers(relative)
        places.append([placement(relative, slots, k, capacity) for k in range(groups)])

    def place(batch, row, stay_ref, cross_ref, value, part):
        stay_ref[row, :, part] = dot(places[batch][0], value, 0, 0).astype(jnp.bfloat16)
        for k in range(1, groups):
            there = dot(places[batch][k], value, 0, 0).astype(jnp.bfloat16)
            cross_ref[k - 1, row, :, part] = there

    parts = [
        slice(start, start + step) for start in range(0, acts_first_ref.shape[1], step)
    ]
    for copy in copies[:2]:
        copy.wait()
    inverse_rms = inverse_rms_of(acts_second_ref, step)
    for part in parts:
        normed = acts_second_ref[:, part].astype(jnp.float32) * inverse_rms * gain_second_ref[:, part]
        place(1, 0, stay_second_ref, cross_second_ref, normed.astype(jnp.bfloat16), part)
    copies[2].wait()
    for part in parts:
        scaled = weight * grad_ref[:, part].astype(jnp.float32)
        place(1, 1, stay_second_ref, cross_second_ref, scaled.astype(jnp.bfloat16), part)
    for copy in copies[3:]:
        copy.wait()
    inverse_rms = inverse_rms_of(acts_first_ref, step)
    for part in parts:
        normed = acts_first_ref[:, part].astype(jnp.float32) * inverse_rms * gain_first_ref[:, part]
        place(0, 0, stay_first_ref, cross_first_ref, normed.astype(jnp.bfloat16), part)


def prepare(groups, capacity, step, route_first, route_second, weight, *large):
    width = large[0].shape[1]
    shape = jax.ShapeDtypeStruct
    return pl.pallas_call(
        functools.partial(prepare_body, groups, capacity, step),
        in_specs=[WHOLE] * 3 + [pl.BlockSpec(memory_space=pl.ANY)] * 5,
        out_specs=[WHOLE] * 4,
        out_shape=[
            shape((1, capacity, width), jnp.bfloat16),
            shape((2, capacity, width), jnp.bfloat16),
            shape((groups - 1, 1, capacity, width), jnp.bfloat16),
            shape((groups - 1, 2, capacity, width), jnp.bfloat16),
        ],
        scratch_shapes=[pltpu.VMEM(array.shape, array.dtype) for array in large]
        + [pltpu.SemaphoreType.DMA((5,))],
        compiler_params=pltpu.CompilerParams(vmem_limit_bytes=PREPARE_LIMIT),
    )(route_first, route_second, weight, *large)


def backward_hidden_body(pieces, *refs):
    rows_refs = refs[:pieces]
    up_refs, down_refs = refs[pieces : pieces + 2], refs[pieces + 2 : pieces + 4]
    back_ref, upper_total, hidden_total = refs[pieces + 4 :]
    step, steps = pl.program_id(0), pl.num_programs(0)
    normed = jnp.concatenate([ref[0] for ref in rows_refs], axis=0)
    scaled = jnp.concatenate([ref[1] for ref in rows_refs], axis=0)
    hidden = up_refs[0].shape[1]

    @pl.when(step == 0)
    def _():
        upper_total[...] = jnp.zeros_like(upper_total)
        hidden_total[...] = jnp.zeros_like(hidden_total)

    for lane in range(2):
        part = slice(lane * hidden, (lane + 1) * hidden)
        upper_total[:, part] += dot(normed, up_refs[lane][...], 1, 0)
        hidden_total[:, part] += dot(scaled, down_refs[lane][...], 1, 1)

    @pl.when(step == steps - 1)
    def _():
        upper = upper_total[...]
        sigmoid = jax.nn.sigmoid(upper)
        back = hidden_total[...] * sigmoid * (1.0 + upper * (1.0 - sigmoid))
        back_ref[...] = back.astype(jnp.bfloat16)


def forward_hidden_body(pieces, *refs):
    rows_refs = refs[:pieces]
    up_refs = refs[pieces : pieces + 2]
    hidden_ref, upper_total = refs[pieces + 2 :]
    step, steps = pl.program_id(0), pl.num_programs(0)
    normed = jnp.concatenate([ref[0] for ref in rows_refs], axis=0)
    hidden = up_refs[0].shape[1]

    @pl.when(step == 0)
    def _():
        upper_total[...] = jnp.zeros_like(upper_total)

    for lane in range(2):
        part = slice(lane * hidden, (lane + 1) * hidden)
        upper_total[:, part] += dot(normed, up_refs[lane][...], 1, 0)

    @pl.when(step == steps - 1)
    def _():
        upper = upper_total[...]
        hidden_ref[...] = (upper * jax.nn.sigmoid(upper)).astype(jnp.bfloat16)


def spread_body(weights_dim, own_rows, hidden_ref, one_ref, other_ref, own_ref, away_ref):
    hidden = hidden_ref.shape[1] // 2
    contract = 1 if weights_dim == 0 else 0
    total = dot(hidden_ref[:, :hidden], one_ref[...], 1, contract)
    total = total + dot(hidden_ref[:, hidden:], other_ref[...], 1, contract)
    own_ref[...] = total[:own_rows]
    away_ref[...] = total[own_rows:].astype(jnp.bfloat16)


def spread(hidden_rows, one, other, weights_dim, first, length, step):
    own_rows = hidden_rows.shape[0] // 2
    offset = first // step
    if weights_dim == 0:
        block, index = (step, one.shape[1]), lambda j: (j + offset, 0)
    else:
        block, index = (one.shape[0], step), lambda j: (0, j + offset)
    return pl.pallas_call(
        functools.partial(spread_body, weights_dim, own_rows),
        grid=(length // step,),
        in_specs=[
            pl.BlockSpec(hidden_rows.shape, lambda j: (0, 0)),
            pl.BlockSpec(block, index),
            pl.BlockSpec(block, index),
        ],
        out_specs=[pl.BlockSpec((own_rows, step), lambda j: (0, j))] * 2,
        out_shape=[
            jax.ShapeDtypeStruct((own_rows, length), jnp.float32),
            jax.ShapeDtypeStruct((own_rows, length), jnp.bfloat16),
        ],
        compiler_params=PARAMS,
    )(hidden_rows, one, other)


def away_placement(relative, groups, capacity):
    away = (groups - 1) * capacity
    columns = lax.broadcasted_iota(jnp.int32, (relative.shape[0], away), 1)
    inside = jnp.where(relative > 0, (relative - 1) * capacity + slot_numbers(relative), -1)
    return jnp.where(inside == columns, 1.0, 0.0).astype(jnp.bfloat16)


def collected(relative, groups, capacity, own, partner, returned):
    slots = slot_numbers(relative)
    stay = own + partner.astype(jnp.float32)
    high = stay.astype(jnp.bfloat16)
    low = (stay - high.astype(jnp.float32)).astype(jnp.bfloat16)
    here = placement(relative, slots, 0, capacity)
    total = dot(here, high, 1, 0) + dot(here, low, 1, 0)
    return total + dot(away_placement(relative, groups, capacity), returned, 1, 0)


def finish_stay_body(
    groups, capacity, step, route_ref, weight_ref, acts_ref, own_ref, partner_ref, *out_refs
):
    relative = relative_groups(route_ref, groups)
    here = placement(relative, slot_numbers(relative), 0, capacity)
    weight = as_column(weight_ref[...])
    for start in range(0, acts_ref.shape[1], step):
        part = slice(start, start + step)
        stay = own_ref[:, part] + partner_ref[:, part].astype(jnp.float32)
        high = stay.astype(jnp.bfloat16)
        low = (stay - high.astype(jnp.float32)).astype(jnp.bfloat16)
        total = dot(here, high, 1, 0) + dot(here, low, 1, 0)
        out = acts_ref[:, part].astype(jnp.float32) + weight * total
        length = out_refs[0].shape[1]
        first = start % length
        out_refs[start // length][:, first : first + step] = out.astype(jnp.bfloat16)


def finish_came_body(groups, capacity, part, pieces, notes_ref, returned_ref, *refs):
    out_hbm, out_ref, sem = refs[-3:]
    relative = relative_groups(notes_ref.at[0:1], groups)
    there = away_placement(relative, groups, capacity)
    weight = as_column(notes_ref[1:2])
    width = out_ref.shape[1] // pieces
    for n, stayed_ref in enumerate(refs[:pieces]):
        piece = slice(n * width, (n + 1) * width)
        total = dot(there, returned_ref[:, piece], 1, 0)
        out = stayed_ref[...].astype(jnp.float32) + weight * total
        out_ref[:, piece] = out.astype(jnp.bfloat16)
    copy = pltpu.make_async_copy(out_ref, out_hbm.at[:, part], sem)
    copy.start()
    copy.wait()


def finish_second_body(
    groups,
    capacity,
    step,
    route_ref,
    acts_ref,
    grad_ref,
    gain_ref,
    own_ref,
    partner_ref,
    returned_ref,
    out_ref,
    gained,
):
    width = acts_ref.shape[1]
    relative = relative_groups(route_ref, groups)
    inverse_rms = inverse_rms_of(acts_ref, step)
    along = 0.0
    for start in range(0, width, step):
        part = slice(start, start + step)
        total = collected(
            relative, groups, capacity, own_ref[:, part], partner_ref[:, part], returned_ref[:, part]
        )
        total = gain_ref[:, part] * total
        gained[:, part] = total
        along = along + jnp.sum(
            acts_ref[:, part].astype(jnp.float32) * total, axis=1, keepdims=True
        )
    scale = inverse_rms * inverse_rms * inverse_rms * (along / width)
    for start in range(0, width, step):
        part = slice(start, start + step)
        values = acts_ref[:, part].astype(jnp.float32)
        out = grad_ref[:, part].astype(jnp.float32) + inverse_rms * gained[:, part] - values * scale
        out_ref[:, part] = out.astype(jnp.bfloat16)


def rows_blocks(arrays, step):
    specs = []
    for array in arrays:
        lead = array.shape[:-1]
        specs.append(pl.BlockSpec((*lead, step), lambda j, zeros=(0,) * len(lead): (*zeros, j)))
    return specs


def per_device(
    acts_first,
    route_first,
    weight_first,
    acts_second,
    grad_second,
    route_second,
    weight_second,
    gain_first,
    up_first,
    down_first,
    gain_second,
    up_second,
    down_second,
):
    owners = lax.axis_size("expert")
    groups = owners // SPLIT
    tokens, width = acts_first.shape[1:]
    capacity = 3 * tokens * SPLIT // (2 * owners)
    away = (groups - 1) * capacity
    step = width_step(width)
    hidden = up_first.shape[2]
    bf16 = jnp.bfloat16
    routes = [route.reshape(1, tokens) for route in (route_first, route_second)]
    weights = [weight.reshape(1, tokens) for weight in (weight_first, weight_second)]
    halves = 2 if width // 128 % 2 == 0 else 1
    length = width // halves
    per_half = 2 if length // 128 % 2 == 0 else 1
    piece = length // per_half
    step = width_step(piece)
    parts = [slice(first, first + length) for first in range(0, width, length)]

    def crossed(blocks):
        came = [to_group(blocks[k - 1], k) for k in range(1, groups)]
        return came[0] if groups == 2 else jnp.concatenate(came, axis=1)

    def returned_rows(rows, send=to_group):
        blocks = [
            send(rows[(k - 1) * capacity : k * capacity], groups - k) for k in range(1, groups)
        ]
        return blocks[0] if groups == 2 else jnp.concatenate(blocks, axis=0)

    down_second_other = swapped(down_second[0], 2)
    up_first_other = swapped(up_first[0], 1)
    stay_first, stay_second, cross_first, cross_second = prepare(
        groups,
        capacity,
        step,
        *routes,
        weights[1],
        acts_first[0],
        gain_first,
        acts_second[0],
        gain_second,
        grad_second[0],
    )
    notes = jnp.concatenate([routes[0].astype(jnp.float32), weights[0]])
    notes = shifted(after(notes, up_first_other), "pipe", 1)
    came_second = crossed(cross_second)
    stay_second_other = swapped(after(stay_second, up_first_other), 1)
    up_second_other = swapped(after(up_second[0], up_first_other), 2)
    down_first_other = swapped(after(down_first[0], up_first_other), 1)
    came_second = after(came_second, down_second_other, stay_second_other, notes)
    came_second_other = swapped(came_second, 1)
    came_first = crossed(after(cross_first, up_second_other))
    stay_first_other = swapped(after(stay_first, up_second_other), 2)

    rows = [stay_second, came_second, stay_second_other, came_second_other]
    if capacity % 16:
        rows = [jnp.concatenate(rows, axis=1)]
    both = 2 * (capacity + away)
    back_upper = pl.pallas_call(
        functools.partial(backward_hidden_body, len(rows)),
        grid=(width // step,),
        in_specs=rows_blocks(rows, step)
        + [pl.BlockSpec((step, hidden), lambda j: (j, 0))] * 2
        + [pl.BlockSpec((hidden, step), lambda j: (0, j))] * 2,
        out_specs=pl.BlockSpec((both, 2 * hidden), lambda j: (0, 0)),
        out_shape=jax.ShapeDtypeStruct((both, 2 * hidden), bf16),
        scratch_shapes=[pltpu.VMEM((both, 2 * hidden), jnp.float32)] * 2,
        compiler_params=PARAMS,
    )(*rows, up_second[0], up_second_other, down_second[0], down_second_other)
    own_second, send_second = spread(back_upper, up_second[0], up_second_other, 0, 0, width, step)
    came_part = swapped(send_second[capacity:], 1)
    stay_part = swapped(send_second[:capacity], 1)

    came_first_other = swapped(came_first, 2)

    def first_hidden(rows):
        if capacity % 16:
            rows = [jnp.concatenate(rows, axis=1)]
        count = sum(array.shape[1] for array in rows)
        return pl.pallas_call(
            functools.partial(forward_hidden_body, len(rows)),
            grid=(width // step,),
            in_specs=rows_blocks(rows, step) + [pl.BlockSpec((step, hidden), lambda j: (j, 0))] * 2,
            out_specs=pl.BlockSpec((count, 2 * hidden), lambda j: (0, 0)),
            out_shape=jax.ShapeDtypeStruct((count, 2 * hidden), bf16),
            scratch_shapes=[pltpu.VMEM((count, 2 * hidden), jnp.float32)],
            compiler_params=PARAMS,
        )(*rows, up_first[0], up_first_other)

    weights_down = (down_first[0], down_first_other, 1)
    stay_hidden = first_hidden([after(stay_first, send_second), stay_first_other])
    stay_own, stay_send = spread(stay_hidden, *weights_down, 0, width, step)
    back = (own_second[capacity:] + after(came_part, stay_send).astype(jnp.float32)).astype(bf16)
    returned = returned_rows(back)
    came_hidden = first_hidden([came_first, came_first_other])
    spreads = [
        spread(came_hidden, *weights_down, part.start, length, step) for part in parts
    ]
    came_parts = [swapped(send, 2) for _, send in spreads]
    stay_first_part = swapped(after(stay_send, *came_parts), 2)
    backs = [
        (own + part.astype(jnp.float32)).astype(bf16) for (own, _), part in zip(spreads, came_parts)
    ]
    returned_first = [returned_rows(rows, to_group_ahead) for rows in backs]

    grad_acts = pl.pallas_call(
        functools.partial(finish_second_body, groups, capacity, step),
        in_specs=[WHOLE] * 7,
        out_specs=WHOLE,
        out_shape=jax.ShapeDtypeStruct((tokens, width), bf16),
        scratch_shapes=[pltpu.VMEM((tokens, width), jnp.float32)],
        compiler_params=PARAMS,
    )(
        routes[1],
        acts_second[0],
        grad_second[0],
        gain_second,
        own_second[:capacity],
        stay_part,
        returned,
    )
    next_grad = shifted(grad_acts, "pipe", 1)
    stayed = pl.pallas_call(
        functools.partial(finish_stay_body, groups, capacity, step),
        in_specs=[WHOLE] * 5,
        out_specs=[WHOLE] * (halves * per_half),
        out_shape=[jax.ShapeDtypeStruct((tokens, piece), bf16)] * (halves * per_half),
        compiler_params=PARAMS,
    )(routes[0], weights[0], after(acts_first[0], next_grad), stay_own, stay_first_part)
    stayed = [shifted(part, "pipe", 1) for part in stayed]

    next_first = []
    for n, (part, rows) in enumerate(zip(parts, returned_first)):
        pieces = stayed[n * per_half : (n + 1) * per_half]
        next_first = [
            pl.pallas_call(
                functools.partial(finish_came_body, groups, capacity, part, per_half),
                in_specs=[WHOLE] * (2 + per_half)
                + [pl.BlockSpec(memory_space=pl.ANY)] * len(next_first),
                out_specs=pl.BlockSpec(memory_space=pl.ANY),
                out_shape=jax.ShapeDtypeStruct((tokens, width), bf16),
                scratch_shapes=[pltpu.VMEM((tokens, length), bf16), pltpu.SemaphoreType.DMA],
                input_output_aliases={2 + per_half: 0} if next_first else {},
                compiler_params=PARAMS,
            )(notes, rows, *pieces, *next_first)
        ]
    return (next_first[0][None], next_grad[None])


def solution(mesh):
    in_specs = (
        P("pipe", "expert", None),
        P("pipe", "expert", None),
        P("pipe", "expert", None),
        P("pipe", "expert", None),
        P("pipe", "expert", None),
        P("pipe", "expert", None),
        P("pipe", "expert", None),
        P("pipe", None),
        P("pipe", None, "expert"),
        P("pipe", "expert", None),
        P("pipe", None),
        P("pipe", None, "expert"),
        P("pipe", "expert", None),
    )
    out_specs = (P("pipe", "expert", None), P("pipe", "expert", None))
    return jax.shard_map(
        per_device, mesh=mesh, in_specs=in_specs, out_specs=out_specs, check_vma=False
    )
```
